512 devices in a mesh: grp: 16 (over y, x), slab: 32 (over z, core).
Axes of the slice: x: 4, y: 4, z: 16, core: 2. Of those that a mesh axis runs over, the one named last changes fastest.
Arguments:
- amplitudes: bfloat16 [2048, 16384], P('grp', 'slab'), may hold values from -6 to 6
- integrals: bfloat16 [128, 128, 16384], P('slab', None, 'grp'), may hold values from -0.109375 to 0.109375
- block_irrep: int32 [128], replicated, may hold values from 0 to 7
- slab_irrep: int32 [128], P('slab'), may hold values from 0 to 7
Outputs:
- ladder: bfloat16 [2048, 16384], P('grp', 'slab')
The draws below stay inside these ranges and needn't reach their ends.
Inputs may be any that keep to these rules, and one draw needn't show every extreme that they name: `block_irrep`: pair irrep labels of the point group. `slab_irrep`: pair irrep labels of the point group.
All inputs are finite; a program needn't handle non-finite values.
Results may differ from the reference program's by a relative error of at most 0.001.
Values may be sent and summed in bfloat16 or wider, within the bound.
No kernel may reach another device: no remote copies, remote signals or barrier semaphores. Data moves between devices by JAX's collectives and lax.ppermute only.
A program may use at most 128 MiB of HBM per device.

```python
import math
import jax
import jax.numpy as jnp
import numpy as np
from jax import lax

BLK = 128
SR = 128
NB = 128
NCD = 16384
NIJ = 2048
NSLAB = 128


def set_ends(values, stream_key, low, high):
    dims = values.shape
    spot = [jax.random.randint(jax.random.fold_in(stream_key, axis), (), 0, dims[axis]) for axis in range(len(dims))]
    values = values.at[tuple(spot)].set(low)
    longest = dims.index(max(dims))
    spot[longest] = (spot[longest] + 1) % dims[longest]
    return values.at[tuple(spot)].set(high)


def raised(array, key, source, target, shards_of, factor):
    def block_of(axis_at):
        return (jnp.arange(array.shape[axis_at]) // (array.shape[axis_at] // shards_of)).reshape((-1,) + (1,) * (array.ndim - 1 - axis_at))

    one_side = jax.random.permutation(key, shards_of)[block_of(target)]
    far = (block_of(target) + shards_of // 2) % shards_of
    return jnp.where((block_of(source) == one_side) | (block_of(source) == far), factor * array, array)


def steps_of(stream_key, extent, cuts, low, top_value):
    def one(dim, blocks):
        draws = jax.random.uniform(jax.random.fold_in(jax.random.fold_in(stream_key, 6), dim), (blocks,), jnp.float32, low / len(cuts), top_value / len(cuts))
        return jnp.repeat(jnp.exp(draws), extent[dim] // blocks).reshape((-1,) + (1,) * (len(extent) - dim - 1))

    factor_of = one(*cuts[0])
    for cut in cuts[1:]:
        factor_of = factor_of * one(*cut)
    return factor_of


def rank_table(count, skew):
    loads = [(1 << 20) // math.isqrt(grade ** skew) + 1 for grade in range(1, count + 1)]
    spread = 1 + sum(loads) // (1 << 30)
    return np.cumsum(np.array([max(1, weight // spread) for weight in loads]))


def ranked_ids(own_key, dims, amount, skew):
    grid = rank_table(amount, skew)
    ticket = jax.random.randint(jax.random.fold_in(own_key, 1), dims, 0, int(grid[amount - 1]))
    rank = jnp.searchsorted(jnp.asarray(grid, jnp.int32), ticket, side="right")
    return jax.random.permutation(jax.random.fold_in(own_key, 2), amount)[rank].astype(jnp.int32)


def bell_draw(rng, extent, spread, bound, pieces=(), dtype=jnp.bfloat16):
    factor_of = steps_of(rng, extent, pieces, -0.22, 0.18) if pieces else 1.0
    array = jax.random.normal(rng, extent, jnp.float32) * spread * factor_of
    return jnp.minimum(jnp.maximum(array, -bound), bound).astype(dtype)


def bell_draw_with(key, shape, scale, bound, shards, heavy, dtype=jnp.bfloat16):
    values = scale * jax.random.normal(key, shape, jnp.float32)
    if shards:
        values = values * steps_of(key, shape, shards, -0.22, 0.18)
    return jnp.clip(raised(values, jax.random.fold_in(key, 3), *heavy), -bound, bound).astype(dtype)


def setup_inputs(seed: int = 0) -> dict:
    arg_keys = jax.random.split(jax.random.key(seed), 5)
    return {
        "amplitudes": bell_draw_with(arg_keys[0], (NIJ, NCD), 1.0, 6.0, ((0, 16), (1, 32)), (1, 0, 32, 2.75)),
        "integrals": bell_draw(arg_keys[1], (NSLAB, SR, NCD), (NCD // 6) ** -0.5, 0.109375, ((0, 32), (2, 16))),
        "block_irrep": set_ends(ranked_ids(arg_keys[2], (NB,), 8, 2), jax.random.fold_in(arg_keys[2], 3), 0, 7).astype(jnp.int32),
        "slab_irrep": set_ends(ranked_ids(arg_keys[3], (NSLAB,), 8, 2), jax.random.fold_in(arg_keys[3], 3), 0, 7).astype(jnp.int32),
    }


def reference(amplitudes, integrals, block_irrep, slab_irrep):
    col_irrep = jnp.repeat(block_irrep, BLK)

    def one_slab(args):
        tile, irrep = args
        keep = col_irrep == irrep
        masked = jnp.where(keep[None, :], tile, jnp.zeros_like(tile))
        return jnp.dot(amplitudes, masked.T, preferred_element_type=jnp.float32)

    parts = lax.map(one_slab, (integrals, slab_irrep))
    whole = jnp.transpose(parts, (1, 0, 2)).reshape(NIJ, NSLAB * SR)
    return whole.astype(jnp.bfloat16)
```

```python
import functools

import jax
import jax.numpy as jnp
import numpy as np
from jax import lax
from jax.experimental import pallas as pl
from jax.experimental.pallas import tpu as pltpu
from jax.sharding import Mesh, PartitionSpec as P

BLK = 128
NY, NX, NZ, NC = 4, 4, 16, 2
AXES = ("y", "x", "z", "c")


def moves(target):
    pairs = []
    for source in np.ndindex(NY, NX, NZ, NC):
        to = target(*source)
        pairs.append((int(np.ravel_multi_index(source, (NY, NX, NZ, NC))), int(np.ravel_multi_index(to, (NY, NX, NZ, NC)))))
    return pairs


def ring(size, step):
    return [(i, (i + step) % size) for i in range(size)]


def swap_cores(v):
    return lax.ppermute(v, "c", ring(NC, 1))


def class_gemm_kernel(where_ref, own, other, b0, b1, b2, b3, out):
    core, first = where_ref[0], where_ref[1]
    half = own.shape[2]
    total = jnp.zeros(out.shape, jnp.float32)
    for d, b in enumerate((b0, b1, b2, b3)):
        slot = lax.rem(first - d + 4, 4)
        mine, theirs = own[slot], other[slot]
        low = jnp.where(core == 0, mine, theirs)
        high = jnp.where(core == 0, theirs, mine)
        dims = (((1,), (1,)), ((), ()))
        total += lax.dot_general(low, b[:, :half], dims, preferred_element_type=jnp.float32)
        total += lax.dot_general(high, b[:, half:], dims, preferred_element_type=jnp.float32)
    out[...] = total


def class_gemm(where, own, other, bs):
    slots, rows, half = own.shape
    outs, width = bs[0].shape
    tile = outs // 2
    return pl.pallas_call(
        class_gemm_kernel,
        out_shape=jax.ShapeDtypeStruct((rows, outs), jnp.float32),
        grid_spec=pltpu.PrefetchScalarGridSpec(
            num_scalar_prefetch=1,
            grid=(outs // tile,),
            in_specs=[pl.BlockSpec((slots, rows, half), lambda n, w: (0, 0, 0))] * 2
            + [pl.BlockSpec((tile, width), lambda n, w: (n, 0))] * 4,
            out_specs=pl.BlockSpec((rows, tile), lambda n, w: (0, n)),
        ),
        compiler_params=pltpu.CompilerParams(vmem_limit_bytes=32 << 20),
        cost_estimate=pl.CostEstimate(flops=2 * rows * outs * width * 4, bytes_accessed=6 << 20, transcendentals=0),
    )(where, own, other, *bs)


def local(amplitudes, integrals, block_irrep, slab_irrep):
    y, x, z, c = (lax.axis_index(a) for a in AXES)
    slabs, slab_rows, width = integrals.shape

    parts = [
        lax.ppermute(
            amplitudes, AXES, moves(lambda y, x, z, c, j=j: (y, z % 4, (z + x - 1 + 4 * j) % NZ, c))
        )
        for j in range(4)
    ]

    labels = lax.dynamic_slice_in_dim(block_irrep, (y * NX + x) * (width // BLK), width // BLK, 0)
    keep = jnp.repeat(labels[None, :] == slab_irrep[:, None], BLK, axis=1)
    masked = jnp.where(keep[:, None, :], integrals, jnp.zeros_like(integrals)).reshape(slabs * slab_rows, width)
    bs = [masked] + [lax.ppermute(masked, "y", ring(NY, -d)) for d in range(1, 4)]

    here = jnp.stack(parts)
    classes = [(0, here)] + [(delta, lax.ppermute(here, "z", ring(NZ, -delta))) for delta in (1, -1, 2)]

    sums = []
    for delta, own in classes:
        other = swap_cores(own)
        plane = z + delta
        offset = lax.rem(plane - x + 1 + 2 * NZ, 4) - 1
        first = lax.rem(lax.rem(plane - offset + 2 * NZ, NZ) // 4 - y + 4, 4)
        where = jnp.stack([c, first]).astype(jnp.int32)
        part = class_gemm(where, own, other, bs)
        sums.append(
            lax.ppermute(
                part, AXES, moves(lambda y, x, z, c, delta=delta: (y, (z + delta - x + 1) % 4, z, c))
            )
        )
    return (sums[0] + sums[1] + sums[2] + sums[3]).astype(jnp.bfloat16)


def solution(mesh):
    split = Mesh(mesh.devices.reshape(NY, NX, NZ, NC), AXES)
    grp, slab = ("y", "x"), ("z", "c")
    in_specs = (P(grp, slab), P(slab, None, grp), P(), P(slab))
    return jax.shard_map(local, mesh=split, in_specs=in_specs, out_specs=P(grp, slab), check_vma=False)
```

```python
import jax
import jax.numpy as jnp
import numpy as np
from jax import lax
from jax.experimental import pallas as pl
from jax.experimental.pallas import tpu as pltpu
from jax.sharding import Mesh, PartitionSpec as P

BLK = 128
NY, NX, NZ, NC = 4, 4, 16, 2
AXES = ("y", "x", "z", "c")
FAR_PLANES = [[4 * zh + zl for zh in range(4)] for zl in range(4)]


def moves(target):
    pairs = []
    for source in np.ndindex(NY, NX, NZ, NC):
        to = target(*source)
        pairs.append((int(np.ravel_multi_index(source, (NY, NX, NZ, NC))), int(np.ravel_multi_index(to, (NY, NX, NZ, NC)))))
    return pairs


def spread(i):
    def target(y, x, z, c):
        step = (0, 1, 2 - 4 * c, -1)[(x + i) % 4]
        return (y, z % 4, (z + step) % NZ, c)

    return moves(target)


def gemm_kernel(info, *refs):
    own, other, b, out, total = refs[0:4], refs[4:8], refs[8], refs[9], refs[10]
    rows, half = own[0].shape[1:]
    core = info[0]
    mine = jnp.concatenate([r[0] for r in own])
    theirs = jnp.concatenate([r[0] for r in other])
    low = jnp.where(core == 0, mine, theirs)
    high = jnp.where(core == 0, theirs, mine)
    dims = (((1,), (1,)), ((), ()))
    part = lax.dot_general(low, b[0, :, :half], dims, preferred_element_type=jnp.float32)
    part += lax.dot_general(high, b[0, :, half:], dims, preferred_element_type=jnp.float32)

    @pl.when(pl.program_id(0) == 0)
    def _():
        total[...] = part

    @pl.when(pl.program_id(0) > 0)
    def _():
        total[...] += part

    @pl.when(pl.program_id(0) == 3)
    def _():
        for i in range(4):
            out[info[1 + i]] = total[i * rows : (i + 1) * rows]


def gemm(info, own, other, bs):
    slots, rows, half = own[0].shape
    _, outs, width = bs.shape
    piece = pl.BlockSpec((1, rows, half), lambda k, w: (k, 0, 0))
    return pl.pallas_call(
        gemm_kernel,
        out_shape=jax.ShapeDtypeStruct((4, rows, outs), jnp.float32),
        grid_spec=pltpu.PrefetchScalarGridSpec(
            num_scalar_prefetch=1,
            grid=(slots,),
            in_specs=[piece] * 8 + [pl.BlockSpec((1, outs, width), lambda k, w: (k, 0, 0))],
            out_specs=pl.BlockSpec((4, rows, outs), lambda k, w: (0, 0, 0)),
            scratch_shapes=[pltpu.VMEM((4 * rows, outs), jnp.float32)],
        ),
        compiler_params=pltpu.CompilerParams(vmem_limit_bytes=32 << 20),
        cost_estimate=pl.CostEstimate(
            flops=8 * rows * outs * width * slots, bytes_accessed=9 << 20, transcendentals=0
        ),
    )(info, *own, *other, bs)


def local(amplitudes, integrals, block_irrep, slab_irrep):
    y, x, z, c = (lax.axis_index(a) for a in AXES)
    slabs, slab_rows, width = integrals.shape

    labels = lax.dynamic_slice_in_dim(block_irrep, (y * NX + x) * (width // BLK), width // BLK, 0)
    keep = jnp.repeat(labels[None, :] == slab_irrep[:, None], BLK, axis=1)
    masked = jnp.where(keep[:, None, :], integrals, jnp.zeros_like(integrals)).reshape(slabs * slab_rows, width)
    bs = lax.all_gather(masked, "y", axis=0)

    here = lax.all_gather(amplitudes, "z", axis=0, axis_index_groups=FAR_PLANES)
    own = [lax.ppermute(here, AXES, spread(i)) for i in range(4)]
    other = [lax.ppermute(v, "c", [(0, 1), (1, 0)]) for v in own]

    places = [lax.rem(z - x - i + 8, 4) for i in range(4)]
    info = jnp.stack([c, *places]).astype(jnp.int32)
    parts = gemm(info, own, other, bs)
    parts = lax.all_to_all(parts, "x", split_axis=0, concat_axis=0)
    return parts.sum(0).astype(jnp.bfloat16)


def solution(mesh):
    split = Mesh(mesh.devices.reshape(NY, NX, NZ, NC), AXES)
    grp, slab = ("y", "x"), ("z", "c")
    in_specs = (P(grp, slab), P(slab, None, grp), P(), P(slab))
    return jax.shard_map(local, mesh=split, in_specs=in_specs, out_specs=P(grp, slab), check_vma=False)
```

```python
import functools

import jax
import jax.numpy as jnp
import numpy as np
from jax import lax
from jax.experimental import pallas as pl
from jax.experimental.pallas import tpu as pltpu
from jax.sharding import Mesh, PartitionSpec as P

BLK = 128
NY, NX, NZ, NC = 4, 4, 16, 2
AXES = ("y", "x", "z", "c")
FAR_PLANES = [[4 * zh + zl for zh in range(4)] for zl in range(4)]


def moves(target):
    pairs = []
    for source in np.ndindex(NY, NX, NZ, NC):
        to = target(*source)
        pairs.append((int(np.ravel_multi_index(source, (NY, NX, NZ, NC))), int(np.ravel_multi_index(to, (NY, NX, NZ, NC)))))
    return pairs


def ring(size, step):
    return [(i, (i + step) % size) for i in range(size)]


def spread(k):
    def target(y, x, z, c):
        step = (0, 1, 2 if z % 2 == 0 else -2, -1)[(x - 2 * z + 2 * c + k) % 4]
        return (y, z % 4, (z + step) % NZ, c)

    return moves(target)


def home(k, cross):
    return moves(lambda y, x, z, c: (y, (z + x - 2 * c - k) % 4, z, c ^ cross))


def matched(b, info, blocks_at, start, count):
    return jnp.concatenate(
        [
            jnp.concatenate(
                [
                    jnp.where(
                        info[blocks_at + k] == info[2 + s],
                        b[s * BLK : (s + 1) * BLK, k * BLK : (k + 1) * BLK],
                        jnp.zeros((BLK, BLK), b.dtype),
                    )
                    for k in range(start, start + count)
                ],
                axis=1,
            )
            for s in range(b.shape[0] // BLK)
        ]
    )


def product(info, a, bs):
    slabs, blocks = bs[0].shape[0] // BLK, bs[0].shape[1] // BLK
    total = None
    for d, b in enumerate(bs):
        slot = lax.rem(info[1] + d, NY)
        for half in range(2):
            part = lax.dot_general(
                jnp.concatenate([r[half, slot] for r in a]),
                matched(b, info, 2 + slabs + slot * blocks, half * blocks // 2, blocks // 2),
                (((1,), (1,)), ((), ())),
                preferred_element_type=jnp.float32,
            )
            total = part if total is None else total + part
    return total


def gemm_kernel(info, a0, a1, b0, b1, b2, b3, out0, out1):
    total = product(info, (a0, a1), (b0, b1, b2, b3))
    rows = out0.shape[0]
    out0[...] = total[:rows]
    out1[...] = total[rows:]


def gemm(info, a, bs):
    _, slots, rows, half = a[0].shape
    columns, width = bs[0].shape
    smem, vmem = pl.BlockSpec(memory_space=pltpu.SMEM), pl.BlockSpec(memory_space=pltpu.VMEM)
    return pl.pallas_call(
        gemm_kernel,
        out_shape=[jax.ShapeDtypeStruct((rows, columns), jnp.float32)] * 2,
        in_specs=[smem] + [vmem] * 6,
        out_specs=[vmem] * 2,
        compiler_params=pltpu.CompilerParams(vmem_limit_bytes=16 << 20),
        cost_estimate=pl.CostEstimate(
            flops=4 * rows * columns * width * slots, bytes_accessed=6 << 20, transcendentals=0
        ),
    )(info, *a, *bs)


def local(amplitudes, integrals, block_irrep, slab_irrep):
    y, x, c = (lax.axis_index(a) for a in ("y", "x", "c"))
    slabs, slab_rows, width = integrals.shape

    b0 = integrals.reshape(slabs * slab_rows, width)
    b1 = lax.ppermute(b0, "y", ring(NY, -1))
    b3 = lax.ppermute(b0, "y", ring(NY, 1))

    here = lax.all_gather(amplitudes, "z", axis=0, axis_index_groups=FAR_PLANES)
    here, b0, b1, b3 = lax.optimization_barrier((here, b0, b1, b3))
    b2 = lax.ppermute(b0, "y", ring(NY, 2))
    there = lax.ppermute(here, "c", ring(NC, 1))
    both = jnp.where(c == 0, jnp.stack([here, there]), jnp.stack([there, here]))

    a = [lax.ppermute(both, AXES, spread(k)) for k in range(2)]

    bs = [b0, b1, b2, b3]
    peer_bs = [lax.ppermute(b, "c", ring(NC, 1)) for b in bs]
    peer_irrep = lax.ppermute(slab_irrep, "c", ring(NC, 1))
    column_irreps = lax.dynamic_index_in_dim(block_irrep.reshape(NY, NX, width // BLK), x, 1, keepdims=False)
    place = jnp.stack([c, y]).astype(jnp.int32)
    info, peer_info = (
        jnp.concatenate([place, irreps, column_irreps.reshape(-1)]) for irreps in (slab_irrep, peer_irrep)
    )

    sums = [lax.ppermute(part, AXES, home(k, 0)) for k, part in enumerate(gemm(info, a, bs))]
    sums += [lax.ppermute(part, AXES, home(k, 1)) for k, part in enumerate(gemm(peer_info, a, peer_bs))]
    return (sums[0] + sums[1] + sums[2] + sums[3]).astype(jnp.bfloat16)


def solution(mesh):
    split = Mesh(mesh.devices.reshape(NY, NX, NZ, NC), AXES)
    grp, slab = ("y", "x"), ("z", "c")
    in_specs = (P(grp, slab), P(slab, None, grp), P(), P(slab))
    return jax.shard_map(local, mesh=split, in_specs=in_specs, out_specs=P(grp, slab), check_vma=False)
```

```python
import jax
import jax.numpy as jnp
import numpy as np
from jax import lax
from jax.experimental import pallas as pl
from jax.experimental.pallas import tpu as pltpu
from jax.sharding import Mesh, PartitionSpec as P

BLK = 128
NY, NX, NZ, NC = 4, 4, 16, 2
AXES = ("y", "x", "z", "c")


def moves(target):
    pairs = []
    for source in np.ndindex(NY, NX, NZ, NC):
        to = target(*source)
        pairs.append((int(np.ravel_multi_index(source, (NY, NX, NZ, NC))), int(np.ravel_multi_index(to, (NY, NX, NZ, NC)))))
    return pairs


def ring(size, step):
    return [(i, (i + step) % size) for i in range(size)]


def matched(b, info, blocks_at, start, count):
    return jnp.concatenate(
        [
            jnp.concatenate(
                [
                    jnp.where(
                        info[blocks_at + k] == info[2 + s],
                        b[s * BLK : (s + 1) * BLK, k * BLK : (k + 1) * BLK],
                        jnp.zeros((BLK, BLK), b.dtype),
                    )
                    for k in range(start, start + count)
                ],
                axis=1,
            )
            for s in range(b.shape[0] // BLK)
        ]
    )


def powers_of_two(exponents):
    power = jnp.ones(exponents.shape, jnp.float32)
    for bit in range(7):
        power = jnp.where(lax.shift_right_logical(exponents, bit) & 1 == 1, power * 2.0 ** (1 << bit), power)
    return power


def encode_kernel(a, out):
    rows, width = a.shape
    values = a[...].astype(jnp.float32)
    largest = jnp.max(jnp.abs(values))
    exponents = lax.broadcasted_iota(jnp.int32, (8, 128), 1)
    exponents = jnp.minimum(exponents, 126)
    fits = powers_of_two(exponents) * largest <= 49152.0
    exponent = jnp.max(jnp.where(fits, exponents, 0))
    scale = powers_of_two(jnp.full((8, 128), exponent, jnp.int32))[:1, :1]
    out[:rows] = (values * scale).astype(out.dtype)
    out[rows:] = jnp.full((out.shape[0] - rows, width), exponent.astype(jnp.float32), jnp.float32).astype(out.dtype)


def encode(a):
    rows, width = a.shape
    vmem = pl.BlockSpec(memory_space=pltpu.VMEM)
    return pl.pallas_call(
        encode_kernel,
        out_shape=jax.ShapeDtypeStruct((rows + 8, width), jnp.bfloat16),
        in_specs=[vmem],
        out_specs=vmem,
        compiler_params=pltpu.CompilerParams(vmem_limit_bytes=8 << 20),
        cost_estimate=pl.CostEstimate(flops=4 * rows * width, bytes_accessed=4 * rows * width, transcendentals=0),
    )(a)


def decoded(a, at):
    rows = a.shape[1] - 8
    exponents = a[at, rows:].astype(jnp.float32)[:1].astype(jnp.int32)
    return a[at, :rows] * (1.0 / powers_of_two(exponents)).astype(a.dtype)


def gemm_kernel(info, a, b0, b1, b2, b3, out):
    x, y = info[0], info[1]
    rows = out.shape[1]
    slabs, blocks = b0.shape[0] // BLK, b0.shape[1] // BLK
    total = None
    for d, b in enumerate((b0, b1, b2, b3)):
        slot = lax.rem(y + d, NY)
        for half in range(2):
            pieces = []
            for g in range(NX):
                plane = lax.rem(4 * slot + x + g + NZ - 1, NZ)
                pieces.append(decoded(a, 2 * plane + half))
            part = lax.dot_general(
                jnp.concatenate(pieces),
                matched(b, info, 2 + slabs + (slot * NX + x) * blocks, half * blocks // 2, blocks // 2),
                (((1,), (1,)), ((), ())),
                preferred_element_type=jnp.float32,
            )
            total = part if total is None else total + part
    for g in range(NX):
        out[g] = total[g * rows : (g + 1) * rows]


def gemm(info, a, bs):
    rows = BLK
    columns, width = bs[0].shape
    smem, vmem = pl.BlockSpec(memory_space=pltpu.SMEM), pl.BlockSpec(memory_space=pltpu.VMEM)
    return pl.pallas_call(
        gemm_kernel,
        out_shape=jax.ShapeDtypeStruct((NX, rows, columns), jnp.float32),
        in_specs=[smem] + [vmem] * 5,
        out_specs=vmem,
        compiler_params=pltpu.CompilerParams(vmem_limit_bytes=16 << 20),
        cost_estimate=pl.CostEstimate(
            flops=8 * rows * columns * width * NY, bytes_accessed=9 << 20, transcendentals=0
        ),
    )(info, a, *bs)


def local(amplitudes, integrals, block_irrep, slab_irrep):
    y, x = lax.axis_index("y"), lax.axis_index("x")
    slabs, slab_rows, width = integrals.shape

    a = encode(amplitudes).astype(jnp.float16)
    a = lax.ppermute(a, AXES, moves(lambda y, x, z, c: (y, z % 4, (z + x - 1) % NZ, c)))

    b0 = integrals.reshape(slabs * slab_rows, width)
    bs = [b0] + [lax.ppermute(b0, "y", ring(NY, -d)) for d in range(1, 4)]

    a = lax.all_gather(a, ("z", "c"), axis=0)
    a = a.astype(jnp.bfloat16)
    info = jnp.concatenate([jnp.stack([x, y]).astype(jnp.int32), slab_irrep, block_irrep])
    parts = gemm(info, a, bs)
    return lax.all_to_all(parts, "x", split_axis=0, concat_axis=0).sum(0).astype(jnp.bfloat16)


def solution(mesh):
    split = Mesh(mesh.devices.reshape(NY, NX, NZ, NC), AXES)
    grp, slab = ("y", "x"), ("z", "c")
    in_specs = (P(grp, slab), P(slab, None, grp), P(), P(slab))
    return jax.shard_map(local, mesh=split, in_specs=in_specs, out_specs=P(grp, slab), check_vma=False)
```

```python
import jax
import jax.numpy as jnp
import numpy as np
from jax import lax
from jax.experimental import pallas as pl
from jax.experimental.pallas import tpu as pltpu
from jax.sharding import Mesh, PartitionSpec as P

BLK = 128
NY, NX, NZ, NC = 4, 4, 16, 2
AXES = ("y", "x", "z", "c")
FINE = 64.0


def moves(target):
    pairs = []
    for source in np.ndindex(NY, NX, NZ, NC):
        to = target(*source)
        pairs.append((int(np.ravel_multi_index(source, (NY, NX, NZ, NC))), int(np.ravel_multi_index(to, (NY, NX, NZ, NC)))))
    return pairs


def ring(size, step):
    return [(i, (i + step) % size) for i in range(size)]


def matched(b, slab_labels, block_labels, blocks_at, start, count):
    return jnp.concatenate(
        [
            jnp.concatenate(
                [
                    jnp.where(
                        block_labels[blocks_at + k] == slab_labels[s],
                        b[s * BLK : (s + 1) * BLK, k * BLK : (k + 1) * BLK],
                        jnp.zeros((BLK, BLK), b.dtype),
                    )
                    for k in range(start, start + count)
                ],
                axis=1,
            )
            for s in range(b.shape[0] // BLK)
        ]
    )


def powers_of_two(exponents):
    power = jnp.ones(exponents.shape, jnp.float32)
    for bit in range(7):
        power = jnp.where(lax.shift_right_logical(exponents, bit) & 1 == 1, power * 2.0 ** (1 << bit), power)
    return power


def encode_kernel(a, out):
    rows, width = a.shape
    values = a[...].astype(jnp.float32)
    largest = jnp.max(jnp.abs(values))
    exponents = lax.broadcasted_iota(jnp.int32, (8, 128), 1)
    exponents = jnp.minimum(exponents, 126)
    fits = powers_of_two(exponents) * largest <= 49152.0
    exponent = jnp.max(jnp.where(fits, exponents, 0))
    scale = powers_of_two(jnp.full((8, 128), exponent, jnp.int32))[:1, :1]
    out[:rows] = (values * scale).astype(out.dtype)
    out[rows:] = jnp.full((out.shape[0] - rows, width), exponent.astype(jnp.float32), jnp.float32).astype(out.dtype)


def encode(a):
    rows, width = a.shape
    vmem = pl.BlockSpec(memory_space=pltpu.VMEM)
    return pl.pallas_call(
        encode_kernel,
        out_shape=jax.ShapeDtypeStruct((rows + 8, width), jnp.bfloat16),
        in_specs=[vmem],
        out_specs=vmem,
        compiler_params=pltpu.CompilerParams(vmem_limit_bytes=8 << 20),
        cost_estimate=pl.CostEstimate(flops=4 * rows * width, bytes_accessed=4 * rows * width, transcendentals=0),
    )(a)


def decoded(a, at):
    rows = a.shape[1] - 8
    exponents = a[at, rows:].astype(jnp.float32)[:1].astype(jnp.int32)
    return a[at, :rows] * (1.0 / powers_of_two(exponents)).astype(a.dtype)


def gemm_kernel(slab_labels, block_labels, a, b0, b1, b2, b3, out):
    x, y = lax.axis_index("x"), lax.axis_index("y")
    rows = out.shape[1]
    blocks = b0.shape[1] // BLK
    total = None
    for d, b in enumerate((b0, b1, b2, b3)):
        slot = lax.rem(y + d, NY)
        for half in range(2):
            pieces = []
            for g in range(NX):
                plane = 4 * slot + lax.rem(x + g, 4)
                pieces.append(decoded(a, 2 * plane + half))
            part = lax.dot_general(
                jnp.concatenate(pieces),
                matched(b, slab_labels, block_labels, (slot * NX + x) * blocks, half * blocks // 2, blocks // 2),
                (((1,), (1,)), ((), ())),
                preferred_element_type=jnp.float32,
            )
            total = part if total is None else total + part
    columns = total.shape[1]
    for g in range(NX):
        block = total[g * rows : (g + 1) * rows]
        largest = jnp.maximum(jnp.max(jnp.abs(block), axis=1, keepdims=True), 2.0**-100)
        exponents = jnp.floor(FINE * (14.99 - jnp.log2(largest)))
        out[g, :, :columns] = jnp.round(block * jnp.exp2(exponents / FINE)).astype(jnp.int32).astype(jnp.int16)
        out[g, :, columns:] = jnp.broadcast_to(exponents, (rows, BLK)).astype(jnp.int32).astype(jnp.int16)


def sum_kernel(parts, out):
    rows, columns = out.shape
    total = jnp.zeros(out.shape, jnp.float32)
    for g in range(NX):
        scale = jnp.exp2(parts[g, :, columns:].astype(jnp.int32).astype(jnp.float32)[:, :1] / -FINE)
        total += parts[g, :, :columns].astype(jnp.int32).astype(jnp.float32) * scale
    out[...] = total.astype(out.dtype)


def summed(parts):
    _, rows, columns = parts.shape
    vmem = pl.BlockSpec(memory_space=pltpu.VMEM)
    return pl.pallas_call(
        sum_kernel,
        out_shape=jax.ShapeDtypeStruct((rows, columns - BLK), jnp.bfloat16),
        in_specs=[vmem],
        out_specs=vmem,
        compiler_params=pltpu.CompilerParams(vmem_limit_bytes=8 << 20),
        cost_estimate=pl.CostEstimate(flops=8 * rows * columns, bytes_accessed=10 * rows * columns, transcendentals=0),
    )(parts)


def gemm(slab_labels, block_labels, a, bs):
    rows = BLK
    columns, width = bs[0].shape
    smem, vmem = pl.BlockSpec(memory_space=pltpu.SMEM), pl.BlockSpec(memory_space=pltpu.VMEM)
    return pl.pallas_call(
        gemm_kernel,
        out_shape=jax.ShapeDtypeStruct((NX, rows, columns + BLK), jnp.int16),
        in_specs=[smem] * 2 + [vmem] * 5,
        out_specs=vmem,
        compiler_params=pltpu.CompilerParams(vmem_limit_bytes=16 << 20),
        cost_estimate=pl.CostEstimate(
            flops=8 * rows * columns * width * NY, bytes_accessed=9 << 20, transcendentals=0
        ),
    )(slab_labels, block_labels, a, *bs)


def local(amplitudes, integrals, block_irrep, slab_irrep):
    slabs, slab_rows, width = integrals.shape

    a = encode(amplitudes).astype(jnp.float16)
    a = lax.ppermute(a, AXES, moves(lambda y, x, z, c: (y, z % 4, z // 4 * 4 + (z + x) % 4, c)))

    b0 = integrals.reshape(slabs * slab_rows, width)
    bs = [b0] + [lax.ppermute(b0, "y", ring(NY, -d)) for d in range(1, 4)]

    a = lax.all_gather(a, ("z", "c"), axis=0)
    a = a.astype(jnp.bfloat16)
    parts = gemm(slab_irrep, block_irrep, a, bs)
    return summed(lax.all_to_all(parts, "x", split_axis=0, concat_axis=0))


def solution(mesh):
    split = Mesh(mesh.devices.reshape(NY, NX, NZ, NC), AXES)
    grp, slab = ("y", "x"), ("z", "c")
    in_specs = (P(grp, slab), P(slab, None, grp), P(), P(slab))
    return jax.shard_map(local, mesh=split, in_specs=in_specs, out_specs=P(grp, slab), check_vma=False)
```

```python
import jax
import jax.numpy as jnp
import numpy as np
from jax import lax
from jax.experimental import pallas as pl
from jax.experimental.pallas import tpu as pltpu
from jax.sharding import Mesh, PartitionSpec as P

BLK = 128
NY, NX, NZ, NC = 4, 4, 16, 2
AXES = ("y", "x", "z", "c")
FINE = 64.0


def moves(target):
    pairs = []
    for source in np.ndindex(NY, NX, NZ, NC):
        to = target(*source)
        pairs.append((int(np.ravel_multi_index(source, (NY, NX, NZ, NC))), int(np.ravel_multi_index(to, (NY, NX, NZ, NC)))))
    return pairs


def ring(size, step):
    return [(i, (i + step) % size) for i in range(size)]


def matched(b, slab_labels, block_labels, blocks_at, start, count):
    return jnp.concatenate(
        [
            jnp.concatenate(
                [
                    jnp.where(
                        block_labels[blocks_at + k] == slab_labels[s],
                        b[s * BLK : (s + 1) * BLK, k * BLK : (k + 1) * BLK],
                        jnp.zeros((BLK, BLK), b.dtype),
                    )
                    for k in range(start, start + count)
                ],
                axis=1,
            )
            for s in range(b.shape[0] // BLK)
        ]
    )


def powers_of_two(exponents):
    power = jnp.ones(exponents.shape, jnp.float32)
    for bit in range(7):
        power = jnp.where(lax.shift_right_logical(exponents, bit) & 1 == 1, power * 2.0 ** (1 << bit), power)
    return power


def encode_kernel(a, out):
    rows, width = a.shape
    values = a[...].astype(jnp.float32)
    largest = jnp.max(jnp.abs(values))
    exponents = lax.broadcasted_iota(jnp.int32, (8, 128), 1)
    exponents = jnp.minimum(exponents, 126)
    fits = powers_of_two(exponents) * largest <= 49152.0
    exponent = jnp.max(jnp.where(fits, exponents, 0))
    scale = powers_of_two(jnp.full((8, 128), exponent, jnp.int32))[:1, :1]
    out[:rows] = (values * scale).astype(out.dtype)
    out[rows:] = jnp.full((out.shape[0] - rows, width), exponent.astype(jnp.float32), jnp.float32).astype(out.dtype)


def encode(a):
    rows, width = a.shape
    vmem = pl.BlockSpec(memory_space=pltpu.VMEM)
    return pl.pallas_call(
        encode_kernel,
        out_shape=jax.ShapeDtypeStruct((rows + 8, width), jnp.bfloat16),
        in_specs=[vmem],
        out_specs=vmem,
        compiler_params=pltpu.CompilerParams(vmem_limit_bytes=8 << 20),
        cost_estimate=pl.CostEstimate(flops=4 * rows * width, bytes_accessed=4 * rows * width, transcendentals=0),
    )(a)


def decoded(a, at):
    rows = a.shape[1] - 8
    exponents = a[at, rows:].astype(jnp.float32)[:1].astype(jnp.int32)
    return a[at, :rows] * (1.0 / powers_of_two(exponents)).astype(a.dtype)


def gemm_kernel(slab_labels, block_labels, a, b0, b1, b2, b3, out):
    x, y = lax.axis_index("x"), lax.axis_index("y")
    rows = out.shape[1]
    blocks = b0.shape[1] // BLK
    total = None
    for d, b in enumerate((b0, b1, b2, b3)):
        slot = lax.rem(y + d, NY)
        for half in range(2):
            pieces = []
            for g in range(NX):
                plane = 4 * slot + lax.rem(x + g, 4)
                pieces.append(decoded(a, 2 * plane + half))
            part = lax.dot_general(
                jnp.concatenate(pieces),
                matched(b, slab_labels, block_labels, (slot * NX + x) * blocks, half * blocks // 2, blocks // 2),
                (((1,), (1,)), ((), ())),
                preferred_element_type=jnp.float32,
            )
            total = part if total is None else total + part
    columns = total.shape[1]
    for g in range(NX):
        block = total[g * rows : (g + 1) * rows]
        largest = jnp.maximum(jnp.max(jnp.abs(block), axis=1, keepdims=True), 2.0**-100)
        exponents = jnp.floor(FINE * (14.99 - jnp.log2(largest)))
        out[g, :, :columns] = jnp.round(block * jnp.exp2(exponents / FINE)).astype(jnp.int32).astype(jnp.int16)
        out[g, :, columns:] = jnp.broadcast_to(exponents, (rows, BLK)).astype(jnp.int32).astype(jnp.int16)


def sum_kernel(parts, out):
    rows, columns = out.shape
    total = jnp.zeros(out.shape, jnp.float32)
    for g in range(NX):
        scale = jnp.exp2(parts[g, :, columns:].astype(jnp.int32).astype(jnp.float32)[:, :1] / -FINE)
        total += parts[g, :, :columns].astype(jnp.int32).astype(jnp.float32) * scale
    out[...] = total.astype(out.dtype)


def summed(parts):
    _, rows, columns = parts.shape
    vmem = pl.BlockSpec(memory_space=pltpu.VMEM)
    return pl.pallas_call(
        sum_kernel,
        out_shape=jax.ShapeDtypeStruct((rows, columns - BLK), jnp.bfloat16),
        in_specs=[vmem],
        out_specs=vmem,
        compiler_params=pltpu.CompilerParams(vmem_limit_bytes=8 << 20),
        cost_estimate=pl.CostEstimate(flops=8 * rows * columns, bytes_accessed=10 * rows * columns, transcendentals=0),
    )(parts)


def gemm(slab_labels, block_labels, a, bs):
    rows = BLK
    columns, width = bs[0].shape
    smem, vmem = pl.BlockSpec(memory_space=pltpu.SMEM), pl.BlockSpec(memory_space=pltpu.VMEM)
    return pl.pallas_call(
        gemm_kernel,
        out_shape=jax.ShapeDtypeStruct((NX, rows, columns + BLK), jnp.int16),
        in_specs=[smem] * 2 + [vmem] * 5,
        out_specs=vmem,
        compiler_params=pltpu.CompilerParams(vmem_limit_bytes=16 << 20),
        cost_estimate=pl.CostEstimate(
            flops=8 * rows * columns * width * NY, bytes_accessed=9 << 20, transcendentals=0
        ),
    )(slab_labels, block_labels, a, *bs)


def local(amplitudes, integrals, block_irrep, slab_irrep):
    slabs, slab_rows, width = integrals.shape

    a = lax.ppermute(amplitudes, AXES, moves(lambda y, x, z, c: (y, z % 4, z // 4 * 4 + (z + x) % 4, c)))

    b0 = integrals.reshape(slabs * slab_rows, width)
    bs = [b0] + [lax.ppermute(b0, "y", ring(NY, -d)) for d in range(1, 4)]

    a = lax.all_gather(encode(a).astype(jnp.float16), ("z", "c"), axis=0)
    a = a.astype(jnp.bfloat16)
    parts = gemm(slab_irrep, block_irrep, a, bs)
    return summed(lax.all_to_all(parts, "x", split_axis=0, concat_axis=0))


def solution(mesh):
    split = Mesh(mesh.devices.reshape(NY, NX, NZ, NC), AXES)
    grp, slab = ("y", "x"), ("z", "c")
    in_specs = (P(grp, slab), P(slab, None, grp), P(), P(slab))
    return jax.shard_map(local, mesh=split, in_specs=in_specs, out_specs=P(grp, slab), check_vma=False)
```

```python
import jax
import jax.numpy as jnp
import numpy as np
from jax import lax
from jax.experimental import pallas as pl
from jax.experimental.pallas import tpu as pltpu
from jax.sharding import Mesh, PartitionSpec as P

BLK = 128
NY, NX, NZ, NC = 4, 4, 16, 2
AXES = ("y", "x", "z", "c")
FINE = 64.0


def moves(target):
    pairs = []
    for source in np.ndindex(NY, NX, NZ, NC):
        to = target(*source)
        pairs.append((int(np.ravel_multi_index(source, (NY, NX, NZ, NC))), int(np.ravel_multi_index(to, (NY, NX, NZ, NC)))))
    return pairs


def ring(size, step):
    return [(i, (i + step) % size) for i in range(size)]


def matched(b, slab_labels, block_labels, blocks_at, start, count):
    return jnp.concatenate(
        [
            jnp.concatenate(
                [
                    jnp.where(
                        block_labels[blocks_at + k] == slab_labels[s],
                        b[s * BLK : (s + 1) * BLK, k * BLK : (k + 1) * BLK],
                        jnp.zeros((BLK, BLK), b.dtype),
                    )
                    for k in range(start, start + count)
                ],
                axis=1,
            )
            for s in range(b.shape[0] // BLK)
        ]
    )


def powers_of_two(exponents):
    power = jnp.ones(exponents.shape, jnp.float32)
    for bit in range(7):
        power = jnp.where(lax.shift_right_logical(exponents, bit) & 1 == 1, power * 2.0 ** (1 << bit), power)
    return power


def encode_kernel(a, out):
    rows, width = a.shape
    values = a[...].astype(jnp.float32)
    largest = jnp.max(jnp.abs(values))
    exponents = lax.broadcasted_iota(jnp.int32, (8, 128), 1)
    exponents = jnp.minimum(exponents, 126)
    fits = powers_of_two(exponents) * largest <= 49152.0
    exponent = jnp.max(jnp.where(fits, exponents, 0))
    scale = powers_of_two(jnp.full((8, 128), exponent, jnp.int32))[:1, :1]
    out[:rows] = (values * scale).astype(out.dtype)
    out[rows:] = jnp.full((out.shape[0] - rows, width), exponent.astype(jnp.float32), jnp.float32).astype(out.dtype)


def encode(a):
    rows, width = a.shape
    vmem = pl.BlockSpec(memory_space=pltpu.VMEM)
    return pl.pallas_call(
        encode_kernel,
        out_shape=jax.ShapeDtypeStruct((rows + 8, width), jnp.bfloat16),
        in_specs=[vmem],
        out_specs=vmem,
        compiler_params=pltpu.CompilerParams(vmem_limit_bytes=8 << 20),
        cost_estimate=pl.CostEstimate(flops=4 * rows * width, bytes_accessed=4 * rows * width, transcendentals=0),
    )(a)


def decoded(a, at):
    rows = a.shape[1] - 8
    exponents = a[at, rows:].astype(jnp.float32)[:1].astype(jnp.int32)
    return a[at, :rows] * (1.0 / powers_of_two(exponents)).astype(a.dtype)


def gemm_kernel(slab_labels, block_labels, a, b0, b1, b2, b3, out):
    x, y = lax.axis_index("x"), lax.axis_index("y")
    rows = out.shape[1]
    blocks = b0.shape[1] // BLK
    total = None
    for d, b in enumerate((b0, b1, b2, b3)):
        slot = lax.rem(y + d, NY)
        for half in range(2):
            pieces = []
            for g in range(NX):
                plane = 4 * slot + lax.rem(x + g, 4)
                pieces.append(decoded(a, 2 * plane + half))
            part = lax.dot_general(
                jnp.concatenate(pieces),
                matched(b, slab_labels, block_labels, (slot * NX + x) * blocks, half * blocks // 2, blocks // 2),
                (((1,), (1,)), ((), ())),
                preferred_element_type=jnp.float32,
            )
            total = part if total is None else total + part
    columns = total.shape[1]
    for g in range(NX):
        block = total[g * rows : (g + 1) * rows]
        largest = jnp.maximum(jnp.max(jnp.abs(block), axis=1, keepdims=True), 2.0**-100)
        exponents = jnp.floor(FINE * (14.99 - jnp.log2(largest)))
        out[g, :, :columns] = jnp.round(block * jnp.exp2(exponents / FINE)).astype(jnp.int32).astype(jnp.int16)
        out[g, :, columns:] = jnp.broadcast_to(exponents, (rows, BLK)).astype(jnp.int32).astype(jnp.int16)


def sum_kernel(parts, out):
    rows, columns = out.shape
    total = jnp.zeros(out.shape, jnp.float32)
    for g in range(NX):
        scale = jnp.exp2(parts[g, :, columns:].astype(jnp.int32).astype(jnp.float32)[:, :1] / -FINE)
        total += parts[g, :, :columns].astype(jnp.int32).astype(jnp.float32) * scale
    out[...] = total.astype(out.dtype)


def summed(parts):
    _, rows, columns = parts.shape
    vmem = pl.BlockSpec(memory_space=pltpu.VMEM)
    return pl.pallas_call(
        sum_kernel,
        out_shape=jax.ShapeDtypeStruct((rows, columns - BLK), jnp.bfloat16),
        in_specs=[vmem],
        out_specs=vmem,
        compiler_params=pltpu.CompilerParams(vmem_limit_bytes=8 << 20),
        cost_estimate=pl.CostEstimate(flops=8 * rows * columns, bytes_accessed=10 * rows * columns, transcendentals=0),
    )(parts)


def gemm(slab_labels, block_labels, a, bs):
    rows = BLK
    columns, width = bs[0].shape
    smem, vmem = pl.BlockSpec(memory_space=pltpu.SMEM), pl.BlockSpec(memory_space=pltpu.VMEM)
    return pl.pallas_call(
        gemm_kernel,
        out_shape=jax.ShapeDtypeStruct((NX, rows, columns + BLK), jnp.int16),
        in_specs=[smem] * 2 + [vmem] * 5,
        out_specs=vmem,
        compiler_params=pltpu.CompilerParams(vmem_limit_bytes=16 << 20),
        cost_estimate=pl.CostEstimate(
            flops=8 * rows * columns * width * NY, bytes_accessed=9 << 20, transcendentals=0
        ),
    )(slab_labels, block_labels, a, *bs)


def local(amplitudes, integrals, block_irrep, slab_irrep):
    slabs, slab_rows, width = integrals.shape

    a = lax.ppermute(amplitudes, AXES, moves(lambda y, x, z, c: (y, z % 4, z // 4 * 4 + (z + x) % 4, c)))

    b0 = integrals.reshape(slabs * slab_rows, width)
    b2, b1, b3 = (lax.ppermute(b0, "y", ring(NY, -d)) for d in (2, 1, 3))
    bs = [b0, b1, b2, b3]

    a = lax.all_gather(encode(a).astype(jnp.float16), ("z", "c"), axis=0)
    a = a.astype(jnp.bfloat16)
    parts = gemm(slab_irrep, block_irrep, a, bs)
    return summed(lax.all_to_all(parts, "x", split_axis=0, concat_axis=0))


def solution(mesh):
    split = Mesh(mesh.devices.reshape(NY, NX, NZ, NC), AXES)
    grp, slab = ("y", "x"), ("z", "c")
    in_specs = (P(grp, slab), P(slab, None, grp), P(), P(slab))
    return jax.shard_map(local, mesh=split, in_specs=in_specs, out_specs=P(grp, slab), check_vma=False)
```

```python
import jax
import jax.numpy as jnp
import numpy as np
from jax import lax
from jax.experimental import pallas as pl
from jax.experimental.pallas import tpu as pltpu
from jax.sharding import Mesh, PartitionSpec as P

BLK = 128
NY, NX, NZ, NC = 4, 4, 16, 2
AXES = ("y", "x", "z", "c")
FINE = 64.0


def moves(target):
    pairs = []
    for source in np.ndindex(NY, NX, NZ, NC):
        to = target(*source)
        pairs.append((int(np.ravel_multi_index(source, (NY, NX, NZ, NC))), int(np.ravel_multi_index(to, (NY, NX, NZ, NC)))))
    return pairs


def ring(size, step):
    return [(i, (i + step) % size) for i in range(size)]


def matched(b, slab_labels, block_labels, blocks_at, start, count):
    return jnp.concatenate(
        [
            jnp.concatenate(
                [
                    jnp.where(
                        block_labels[blocks_at + k] == slab_labels[s],
                        b[s * BLK : (s + 1) * BLK, k * BLK : (k + 1) * BLK],
                        jnp.zeros((BLK, BLK), b.dtype),
                    )
                    for k in range(start, start + count)
                ],
                axis=1,
            )
            for s in range(b.shape[0] // BLK)
        ]
    )


def powers_of_two(exponents):
    power = jnp.ones(exponents.shape, jnp.float32)
    for bit in range(7):
        power = jnp.where(lax.shift_right_logical(exponents, bit) & 1 == 1, power * 2.0 ** (1 << bit), power)
    return power


def encode_kernel(a, out):
    rows, width = a.shape
    values = a[...].astype(jnp.float32)
    largest = jnp.max(jnp.abs(values))
    exponents = lax.broadcasted_iota(jnp.int32, (8, 128), 1)
    exponents = jnp.minimum(exponents, 126)
    fits = powers_of_two(exponents) * largest <= 49152.0
    exponent = jnp.max(jnp.where(fits, exponents, 0))
    scale = powers_of_two(jnp.full((8, 128), exponent, jnp.int32))[:1, :1]
    out[:rows] = (values * scale).astype(out.dtype)
    out[rows:] = jnp.full((out.shape[0] - rows, width), exponent.astype(jnp.float32), jnp.float32).astype(out.dtype)


def encode(a):
    rows, width = a.shape
    vmem = pl.BlockSpec(memory_space=pltpu.VMEM)
    return pl.pallas_call(
        encode_kernel,
        out_shape=jax.ShapeDtypeStruct((rows + 8, width), jnp.bfloat16),
        in_specs=[vmem],
        out_specs=vmem,
        compiler_params=pltpu.CompilerParams(vmem_limit_bytes=8 << 20),
        cost_estimate=pl.CostEstimate(flops=4 * rows * width, bytes_accessed=4 * rows * width, transcendentals=0),
    )(a)


def decoded(a, at):
    rows = a.shape[1] - 8
    exponents = a[at, rows:].astype(jnp.float32)[:1].astype(jnp.int32)
    return a[at, :rows] * (1.0 / powers_of_two(exponents)).astype(a.dtype)


def gemm_kernel(slab_labels, block_labels, a, b0, b1, b2, b3, out):
    x, y = lax.axis_index("x"), lax.axis_index("y")
    rows = out.shape[1]
    blocks = b0.shape[1] // BLK
    total = None
    for d, b in enumerate((b0, b1, b2, b3)):
        slot = lax.rem(y + d, NY)
        for half in range(2):
            pieces = []
            for g in range(NX):
                plane = 4 * slot + lax.rem(x + g, 4)
                pieces.append(decoded(a, 2 * plane + half))
            part = lax.dot_general(
                jnp.concatenate(pieces),
                matched(b, slab_labels, block_labels, (slot * NX + x) * blocks, half * blocks // 2, blocks // 2),
                (((1,), (1,)), ((), ())),
                preferred_element_type=jnp.float32,
            )
            total = part if total is None else total + part
    columns = total.shape[1]
    for g in range(NX):
        block = total[g * rows : (g + 1) * rows]
        largest = jnp.maximum(jnp.max(jnp.abs(block), axis=1, keepdims=True), 2.0**-100)
        exponents = jnp.floor(FINE * (14.99 - jnp.log2(largest)))
        out[g, :, :columns] = jnp.round(block * jnp.exp2(exponents / FINE)).astype(jnp.int32).astype(jnp.int16)
        out[g, :, columns:] = jnp.broadcast_to(exponents, (rows, BLK)).astype(jnp.int32).astype(jnp.int16)


def sum_kernel(parts, out):
    rows, columns = out.shape
    total = jnp.zeros(out.shape, jnp.float32)
    for g in range(NX):
        scale = jnp.exp2(parts[g, :, columns:].astype(jnp.int32).astype(jnp.float32)[:, :1] / -FINE)
        total += parts[g, :, :columns].astype(jnp.int32).astype(jnp.float32) * scale
    out[...] = total.astype(out.dtype)


def summed(parts):
    _, rows, columns = parts.shape
    vmem = pl.BlockSpec(memory_space=pltpu.VMEM)
    return pl.pallas_call(
        sum_kernel,
        out_shape=jax.ShapeDtypeStruct((rows, columns - BLK), jnp.bfloat16),
        in_specs=[vmem],
        out_specs=vmem,
        compiler_params=pltpu.CompilerParams(vmem_limit_bytes=8 << 20),
        cost_estimate=pl.CostEstimate(flops=8 * rows * columns, bytes_accessed=10 * rows * columns, transcendentals=0),
    )(parts)


def gemm(slab_labels, block_labels, a, bs):
    rows = BLK
    columns, width = bs[0].shape
    smem, vmem = pl.BlockSpec(memory_space=pltpu.SMEM), pl.BlockSpec(memory_space=pltpu.VMEM)
    return pl.pallas_call(
        gemm_kernel,
        out_shape=jax.ShapeDtypeStruct((NX, rows, columns + BLK), jnp.int16),
        in_specs=[smem] * 2 + [vmem] * 5,
        out_specs=vmem,
        compiler_params=pltpu.CompilerParams(vmem_limit_bytes=16 << 20),
        cost_estimate=pl.CostEstimate(
            flops=8 * rows * columns * width * NY, bytes_accessed=9 << 20, transcendentals=0
        ),
    )(slab_labels, block_labels, a, *bs)


def local(amplitudes, integrals, block_irrep, slab_irrep):
    slabs, slab_rows, width = integrals.shape

    a = lax.ppermute(amplitudes, AXES, moves(lambda y, x, z, c: (y, z % 4, z // 4 * 4 + (z + x) % 4, c)))

    b0 = integrals.reshape(slabs * slab_rows, width)
    b1, b3, b2 = (lax.ppermute(b0, "y", ring(NY, -d)) for d in (1, 3, 2))
    bs = [b0, b1, b2, b3]

    a = lax.all_gather(encode(a).astype(jnp.float16), ("z", "c"), axis=0)
    a = a.astype(jnp.bfloat16)
    parts = gemm(slab_irrep, block_irrep, a, bs)
    return summed(lax.all_to_all(parts, "x", split_axis=0, concat_axis=0))


def solution(mesh):
    split = Mesh(mesh.devices.reshape(NY, NX, NZ, NC), AXES)
    grp, slab = ("y", "x"), ("z", "c")
    in_specs = (P(grp, slab), P(slab, None, grp), P(), P(slab))
    return jax.shard_map(local, mesh=split, in_specs=in_specs, out_specs=P(grp, slab), check_vma=False)
```
